32 devices in a mesh: seq: 8 (over y, x, core), fsdp: 4 (over z).
Axes of the slice: x: 2, y: 2, z: 4, core: 2. Of those that a mesh axis runs over, the one named last changes fastest.
Arguments:
- latents: bfloat16 [8, 256, 3072], P('seq', None, 'fsdp'), may hold values from -6 to 6
- spatial_qkv: bfloat16 [3, 8, 256, 2048], P(None, 'seq', None, 'fsdp'), may hold values from -160 to 160
- spatial_out: bfloat16 [3072, 2048], P('seq', 'fsdp'), may hold values from -0.125 to 0.125
- temporal_qkv: bfloat16 [3072, 6144], P('seq', 'fsdp'), may hold values from -1.4072913 to 1.4072913
- temporal_out: bfloat16 [3072, 2048], P('seq', 'fsdp'), may hold values from -0.125 to 0.125
- mlp_in: bfloat16 [3072, 12288], P('seq', 'fsdp'), may hold values from -0.109375 to 0.109375
- mlp_out: bfloat16 [3072, 12288], P('seq', 'fsdp'), may hold values from -0.0546875 to 0.0546875
- upstream: bfloat16 [8, 256, 3072], P('seq'), may hold values from -6 to 6
Outputs:
- block_out: bfloat16 [8, 256, 3072], P('seq', None, 'fsdp')
- grad_latents: bfloat16 [8, 256, 3072], P('seq', None, 'fsdp')
- grad_spatial_qkv: bfloat16 [3, 8, 256, 2048], P(None, 'seq', None, 'fsdp')
- grad_spatial_out: float32 [3072, 2048], P('seq', 'fsdp')
- grad_temporal_qkv: float32 [3072, 6144], P('seq', 'fsdp')
- grad_temporal_out: float32 [3072, 2048], P('seq', 'fsdp')
- grad_mlp_in: float32 [3072, 12288], P('seq', 'fsdp')
- grad_mlp_out: float32 [3072, 12288], P('seq', 'fsdp')
The draws below stay inside these ranges and needn't reach their ends.
All inputs are finite; a program needn't handle non-finite values.
Results may differ from the reference program's by a relative error of at most 0.03.
Values may be sent and summed in bfloat16 or wider, within the bound.
A program may use at most 192 MiB of HBM per device.

```python
import jax
import jax.numpy as jnp
from jax import lax

D = 3072
HEADS = 16
HD = 128
FF = 12288
PATCH = 256
FRAMES = 8
N_SEQ = 8
N_FSDP = 4


def draw_spatial_qkv(key, part):
    key = jax.random.fold_in(key, 11)
    first = jax.random.fold_in(key, 0)
    base = jnp.clip(jax.random.normal(first, (3, FRAMES, PATCH, HEADS * HD), jnp.float32), -6.0, 6.0)
    return base.astype(jnp.bfloat16)


def draw_temporal_qkv(key, part):
    key = jax.random.fold_in(key, 23)
    first = jax.random.fold_in(key, 0)
    base = jnp.clip(jax.random.normal(first, (D, HEADS, 3, HD), jnp.float32), -6.0, 6.0) * D ** (-0.5)
    return base.reshape(D, HEADS * 3 * HD).astype(jnp.bfloat16)


def levels(rng, extent, shards, least, top_value):
    level, own = 1.0, jax.random.fold_in(rng, 6)
    for axis_at, blocks in shards:
        steps = jnp.exp(jax.random.uniform(jax.random.fold_in(own, axis_at), (blocks,), jnp.float32, least / len(shards), top_value / len(shards)))
        level = level * jnp.repeat(steps, extent[axis_at] // blocks).reshape([-1 if axis == axis_at else 1 for axis in range(len(extent))])
    return level


def noise(key, dims, scale, bound, cuts=(), kind=jnp.bfloat16):
    gain = levels(key, dims, cuts, -0.22, 0.18) if cuts else 1.0
    drawn = jax.random.normal(key, dims, jnp.float32) * scale * gain
    return jnp.minimum(jnp.maximum(drawn, -bound), bound).astype(kind)


def setup_inputs(seed: int = 0) -> dict:
    seeds = jax.random.split(jax.random.key(seed), 9)
    latents = noise(seeds[0], (FRAMES, PATCH, D), 1.0, 6.0, ((0, 8), (2, 4)))
    spatial_qkv = draw_spatial_qkv(jax.random.fold_in(seeds[8], 71), 0)
    spatial_out = noise(seeds[2], (D, HEADS * HD), (HEADS * HD) ** -0.5, 0.125, ((0, 8), (1, 4)))
    temporal_qkv = draw_temporal_qkv(jax.random.fold_in(seeds[8], 71), 0)
    temporal_out = noise(seeds[4], (D, HEADS * HD), (HEADS * HD) ** -0.5, 0.125, ((0, 8), (1, 4)))
    mlp_in = noise(seeds[5], (D, FF), D ** -0.5, 0.109375, ((0, 8), (1, 4)))
    mlp_out = noise(seeds[6], (D, FF), FF ** -0.5, 0.0546875, ((0, 8), (1, 4)))
    upstream = noise(seeds[7], (FRAMES, PATCH, D), 1.0, 6.0, ((0, 8),))
    return {"latents": latents, "spatial_qkv": spatial_qkv, "spatial_out": spatial_out, "temporal_qkv": temporal_qkv, "temporal_out": temporal_out, "mlp_in": mlp_in, "mlp_out": mlp_out, "upstream": upstream}


epsilon = 1e-06
grad_scale = 0.015625

def layer_norm(hidden):
    average = lax.optimization_barrier(jnp.mean(hidden, axis=-1, keepdims=True))
    centred = hidden - average
    spread = lax.optimization_barrier(jnp.mean(centred * centred, axis=-1, keepdims=True))
    return centred * lax.rsqrt(spread + epsilon)

def norm_back(hidden, incoming):
    average = lax.optimization_barrier(jnp.mean(hidden, axis=-1, keepdims=True))
    centred = hidden - average
    spread = lax.optimization_barrier(jnp.mean(centred * centred, axis=-1, keepdims=True))
    inverse = lax.rsqrt(spread + epsilon)
    normed = centred * inverse
    return inverse * (incoming - lax.optimization_barrier(jnp.mean(incoming, axis=-1, keepdims=True)) - normed * lax.optimization_barrier(jnp.mean(incoming * normed, axis=-1, keepdims=True)))

def times_t(matrix, factor):
    return lax.dot_general(matrix, factor, (((1,), (1,)), ((), ())), preferred_element_type=jnp.float32)

def left_times(matrix, factor):
    return lax.dot_general(matrix, factor, (((0,), (0,)), ((), ())), preferred_element_type=jnp.float32)

def attend(query_rows, incoming_keys, value_rows):
    attention_logits = jnp.einsum('otw,osw->ots', query_rows.astype(jnp.float32), incoming_keys.astype(jnp.float32)) * query_rows.shape[-1] ** (-0.5)
    attention_probs = jax.nn.softmax(attention_logits, axis=-1).astype(jnp.bfloat16)
    return jnp.einsum('hfj,hjt->hft', attention_probs.astype(jnp.float32), value_rows.astype(jnp.float32)).astype(jnp.bfloat16)

def spatial(triple):
    frames = triple.shape[1]
    patches = triple.shape[2]
    columns = triple.shape[3]
    heads_here = columns // HD
    pieces = triple.reshape(3, frames, patches, heads_here, HD).transpose(0, 1, 3, 2, 4).reshape(3, frames * heads_here, patches, HD)
    result = attend(pieces[0], pieces[1], pieces[2])
    return result.reshape(frames, heads_here, patches, HD).transpose(0, 2, 1, 3).reshape(frames * patches, columns)

def temporal(triple_rows, frames, spot_count):
    heads_here = triple_rows.shape[1] // (3 * HD)
    pieces = triple_rows.reshape(frames, spot_count, heads_here, 3, HD).transpose(3, 1, 2, 0, 4).reshape(3, spot_count * heads_here, frames, HD)
    result = attend(pieces[0], pieces[1], pieces[2])
    return result.reshape(spot_count, heads_here, frames, HD).transpose(2, 0, 1, 3).reshape(frames * spot_count, heads_here * HD)

def smooth(pre_value):
    return jax.nn.gelu(pre_value, approximate=True)

def rounded(term):
    return lax.optimization_barrier(term.astype(jnp.bfloat16)).astype(jnp.float32)

def group_terms(matrix, factor, group_count):
    columns = matrix.shape[1] // group_count
    running = jnp.zeros((matrix.shape[0], factor.shape[0]), jnp.float32)
    for member in range(group_count):
        start = member * columns
        running = running + rounded(times_t(matrix[:, start:start + columns], factor[:, start:start + columns]))
    return running

def group_norm_terms(hidden, matrix, factor, group_count):
    columns = matrix.shape[1] // group_count
    running = jnp.zeros((matrix.shape[0], factor.shape[0]), jnp.float32)
    for member in range(group_count):
        start = member * columns
        product = times_t(matrix[:, start:start + columns], factor[:, start:start + columns])
        running = running + rounded(norm_back(hidden, product))
    return running

def block_partials(matrix, factor, block_count):
    length = matrix.shape[0] // block_count
    running = jnp.zeros((matrix.shape[1], factor.shape[1]), jnp.float32)
    for section in range(block_count):
        start = section * length
        running = running + rounded(left_times(matrix[start:start + length], factor[start:start + length]) * grad_scale)
    return running

def position_order(table, frames, block_count):
    columns = table.shape[1]
    patches = table.shape[0] // frames
    return table.reshape(frames, block_count, patches // block_count, columns).transpose(1, 0, 2, 3).reshape(table.shape[0], columns)

def reference(latents, spatial_qkv, spatial_out, temporal_qkv, temporal_out, mlp_in, mlp_out, upstream):
    row_count = FRAMES * PATCH
    latent_rows = latents.reshape(row_count, D)
    spatial_output, spatial_back = jax.vjp(spatial, spatial_qkv)
    first_mid = lax.optimization_barrier((latent_rows.astype(jnp.float32) + group_terms(spatial_output, spatial_out, N_FSDP)).astype(jnp.bfloat16))
    first_wide = first_mid.astype(jnp.float32)
    first_norm = layer_norm(first_wide).astype(jnp.bfloat16)
    triple_rows = jnp.dot(first_norm, temporal_qkv, preferred_element_type=jnp.float32).astype(jnp.bfloat16)
    temporal_result, temporal_back = jax.vjp(lambda triple: temporal(triple, FRAMES, PATCH), triple_rows)
    second_mid = lax.optimization_barrier((first_wide + group_terms(temporal_result, temporal_out, N_FSDP)).astype(jnp.bfloat16))
    second_wide = second_mid.astype(jnp.float32)
    second_norm = layer_norm(second_wide).astype(jnp.bfloat16)
    hidden_pre = jnp.dot(second_norm, mlp_in, preferred_element_type=jnp.float32)
    hidden_act = smooth(hidden_pre).astype(jnp.bfloat16)
    block_out = (second_wide + group_terms(hidden_act, mlp_out, N_FSDP)).astype(jnp.bfloat16)
    upstream_rows = upstream.reshape(row_count, D)
    act_grad = jnp.dot(upstream_rows, mlp_out, preferred_element_type=jnp.float32)
    pre_grad = jax.vjp(smooth, hidden_pre)[1](act_grad)[0].astype(jnp.bfloat16)
    second_grad = lax.optimization_barrier((upstream_rows.astype(jnp.float32) + group_norm_terms(second_wide, pre_grad, mlp_in, N_FSDP)).astype(jnp.bfloat16))
    temporal_grad = jnp.dot(second_grad, temporal_out, preferred_element_type=jnp.float32).astype(jnp.bfloat16)
    triple_grad = temporal_back(temporal_grad)[0]
    first_back = rounded(group_norm_terms(first_wide, triple_grad, temporal_qkv, N_FSDP))
    first_grad = (second_grad.astype(jnp.float32) + first_back).astype(jnp.bfloat16)
    spatial_grad = jnp.dot(first_grad, spatial_out, preferred_element_type=jnp.float32).astype(jnp.bfloat16)
    grad_spatial_qkv = spatial_back(spatial_grad)[0]
    grad_spatial_out = block_partials(first_grad, spatial_output, N_SEQ)
    grad_temporal_qkv = block_partials(position_order(first_norm, FRAMES, N_SEQ), position_order(triple_grad, FRAMES, N_SEQ), N_SEQ)
    grad_temporal_out = block_partials(second_grad, temporal_result, N_SEQ)
    grad_mlp_in = block_partials(second_norm, pre_grad, N_SEQ)
    grad_mlp_out = block_partials(upstream_rows, hidden_act, N_SEQ)
    return (block_out.reshape(FRAMES, PATCH, D), first_grad.reshape(FRAMES, PATCH, D), grad_spatial_qkv, grad_spatial_out, grad_temporal_qkv, grad_temporal_out, grad_mlp_in, grad_mlp_out)
```

```python
import jax
import jax.numpy as jnp
from jax import lax
from jax.sharding import PartitionSpec as P

HD = 128


epsilon = 1e-06
grad_scale = 0.015625


def layer_norm(hidden):
    average = jnp.mean(hidden, axis=-1, keepdims=True)
    centred = hidden - average
    spread = jnp.mean(centred * centred, axis=-1, keepdims=True)
    return centred * lax.rsqrt(spread + epsilon)


def norm_back(hidden, incoming):
    average = jnp.mean(hidden, axis=-1, keepdims=True)
    centred = hidden - average
    spread = jnp.mean(centred * centred, axis=-1, keepdims=True)
    inverse = lax.rsqrt(spread + epsilon)
    normed = centred * inverse
    return inverse * (
        incoming
        - jnp.mean(incoming, axis=-1, keepdims=True)
        - normed * jnp.mean(incoming * normed, axis=-1, keepdims=True)
    )


def times_t(matrix, factor):
    return lax.dot_general(
        matrix, factor, (((1,), (1,)), ((), ())), preferred_element_type=jnp.float32
    )


def left_times(matrix, factor):
    return (
        lax.dot_general(
            matrix, factor, (((0,), (0,)), ((), ())), preferred_element_type=jnp.float32
        )
        * grad_scale
    )


def attend(query_rows, incoming_keys, value_rows):
    attention_logits = jnp.einsum(
        "otw,osw->ots", query_rows, incoming_keys, preferred_element_type=jnp.float32
    ) * query_rows.shape[-1] ** (-0.5)
    attention_probs = jax.nn.softmax(attention_logits, axis=-1).astype(jnp.bfloat16)
    return jnp.einsum(
        "hfj,hjt->hft", attention_probs, value_rows, preferred_element_type=jnp.float32
    ).astype(jnp.bfloat16)


def spatial(triple):
    frames = triple.shape[1]
    patches = triple.shape[2]
    columns = triple.shape[3]
    heads_here = columns // HD
    pieces = (
        triple.reshape(3, frames, patches, heads_here, HD)
        .transpose(0, 1, 3, 2, 4)
        .reshape(3, frames * heads_here, patches, HD)
    )
    result = attend(pieces[0], pieces[1], pieces[2])
    return (
        result.reshape(frames, heads_here, patches, HD)
        .transpose(0, 2, 1, 3)
        .reshape(frames * patches, columns)
    )


def temporal(triple_rows, frames, spot_count):
    heads_here = triple_rows.shape[1] // (3 * HD)
    pieces = (
        triple_rows.reshape(frames, spot_count, heads_here, 3, HD)
        .transpose(3, 1, 2, 0, 4)
        .reshape(3, spot_count * heads_here, frames, HD)
    )
    result = attend(pieces[0], pieces[1], pieces[2])
    return (
        result.reshape(spot_count, heads_here, frames, HD)
        .transpose(2, 0, 1, 3)
        .reshape(frames * spot_count, heads_here * HD)
    )


def smooth(pre_value):
    return jax.nn.gelu(pre_value, approximate=True)


def fetch_rows(weight):
    return lax.all_gather(weight, "seq", axis=0, tiled=True)


def widen(table):
    copies = jnp.broadcast_to(table[None], (lax.axis_size("fsdp"),) + table.shape)
    return lax.all_to_all(copies, "fsdp", split_axis=0, concat_axis=2, tiled=True)[0]


def head_sum(terms):
    groups = lax.axis_size("fsdp")
    moved = lax.all_to_all(
        terms.astype(jnp.bfloat16), "fsdp", split_axis=1, concat_axis=0, tiled=True
    )
    return jnp.sum(
        moved.reshape(groups, terms.shape[0], terms.shape[1] // groups).astype(jnp.float32), axis=0
    )


def late_sum(terms):
    return lax.psum_scatter(
        terms.astype(jnp.bfloat16), "fsdp", scatter_dimension=1, tiled=True
    ).astype(jnp.float32)


def own_columns(table):
    return lax.all_to_all(table, "seq", split_axis=1, concat_axis=0, tiled=True)


def all_tokens(table):
    return lax.all_gather(table, "seq", axis=0, tiled=True)


def send_rows(grad_part):
    return lax.psum_scatter(
        grad_part.astype(jnp.bfloat16), "seq", scatter_dimension=0, tiled=True
    ).astype(jnp.float32)


def regroup(block):
    return lax.all_to_all(block, "seq", split_axis=0, concat_axis=1, tiled=True)


def to_positions(table, local_frames):
    devices = lax.axis_size("seq")
    row_count = table.shape[0]
    columns = table.shape[1]
    spot_count = row_count // (local_frames * devices)
    block = table.reshape(local_frames, devices, spot_count, columns).transpose(1, 0, 2, 3)
    return regroup(block).reshape(row_count, columns)


def to_frames(table, local_frames):
    devices = lax.axis_size("seq")
    row_count = table.shape[0]
    columns = table.shape[1]
    spot_count = row_count // (local_frames * devices)
    block = table.reshape(devices, local_frames, spot_count, columns)
    moved = regroup(block).reshape(devices, local_frames, spot_count, columns).transpose(1, 0, 2, 3)
    return moved.reshape(row_count, columns)


def body(latents, spatial_qkv, spatial_out, temporal_qkv, temporal_out, mlp_in, mlp_out, upstream):
    local_frames = latents.shape[0]
    patches = latents.shape[1]
    narrow = latents.shape[2]
    devices = lax.axis_size("seq")
    all_frames = local_frames * devices
    spot_count = patches // devices
    row_count = local_frames * patches
    spatial_output, spatial_back = jax.vjp(spatial, spatial_qkv)
    spatial_full = fetch_rows(spatial_out)
    first_mid = (
        latents.reshape(row_count, narrow).astype(jnp.float32)
        + head_sum(times_t(spatial_output, spatial_full))
    ).astype(jnp.bfloat16)
    first_wide = widen(to_positions(first_mid, local_frames)).astype(jnp.float32)
    first_norm = layer_norm(first_wide).astype(jnp.bfloat16)
    triple_full = fetch_rows(temporal_qkv)
    triple_rows = jnp.dot(first_norm, triple_full, preferred_element_type=jnp.float32).astype(
        jnp.bfloat16
    )
    temporal_result, temporal_back = jax.vjp(
        lambda triple: temporal(triple, all_frames, spot_count), triple_rows
    )
    frames_result = to_frames(temporal_result, local_frames)
    out_full = fetch_rows(temporal_out)
    second_mid = (
        first_mid.astype(jnp.float32) + head_sum(times_t(frames_result, out_full))
    ).astype(jnp.bfloat16)
    second_wide = widen(second_mid).astype(jnp.float32)
    second_norm = layer_norm(second_wide).astype(jnp.bfloat16)
    inner_full = fetch_rows(mlp_in)
    hidden_pre = jnp.dot(second_norm, inner_full, preferred_element_type=jnp.float32)
    hidden_act = smooth(hidden_pre).astype(jnp.bfloat16)
    outer_full = fetch_rows(mlp_out)
    block_out = (second_mid.astype(jnp.float32) + late_sum(times_t(hidden_act, outer_full))).astype(
        jnp.bfloat16
    )
    upstream_rows = upstream.reshape(row_count, upstream.shape[2])
    upstream_cols = lax.dynamic_slice_in_dim(
        upstream_rows, lax.axis_index("fsdp") * narrow, narrow, 1
    )
    act_grad = jnp.dot(upstream_rows, outer_full, preferred_element_type=jnp.float32)
    pre_grad = jax.vjp(smooth, hidden_pre)[1](act_grad)[0].astype(jnp.bfloat16)
    second_grad = (
        upstream_cols.astype(jnp.float32)
        + head_sum(norm_back(second_wide, times_t(pre_grad, inner_full)))
    ).astype(jnp.bfloat16)
    second_grad_wide = widen(second_grad)
    temporal_grad = to_positions(
        jnp.dot(second_grad_wide, out_full, preferred_element_type=jnp.float32).astype(
            jnp.bfloat16
        ),
        local_frames,
    )
    triple_grad = temporal_back(temporal_grad)[0]
    first_back = head_sum(norm_back(first_wide, times_t(triple_grad, triple_full))).astype(
        jnp.bfloat16
    )
    first_grad = (
        second_grad.astype(jnp.float32) + to_frames(first_back, local_frames).astype(jnp.float32)
    ).astype(jnp.bfloat16)
    first_grad_wide = widen(first_grad)
    spatial_grad = jnp.dot(
        first_grad_wide, spatial_full, preferred_element_type=jnp.float32
    ).astype(jnp.bfloat16)
    grad_spatial_qkv = spatial_back(spatial_grad)[0]
    grads = (
        send_rows(left_times(first_grad_wide, spatial_output)),
        left_times(own_columns(first_norm), all_tokens(triple_grad)),
        send_rows(left_times(second_grad_wide, frames_result)),
        left_times(own_columns(second_norm), all_tokens(pre_grad)),
        left_times(own_columns(upstream_rows), all_tokens(hidden_act)),
    )
    return (
        block_out.reshape(local_frames, patches, narrow),
        first_grad.reshape(local_frames, patches, narrow),
        grad_spatial_qkv,
        grads[0],
        grads[1],
        grads[2],
        grads[3],
        grads[4],
    )


def solution(mesh):
    in_specs = (
        P("seq", None, "fsdp"),
        P(None, "seq", None, "fsdp"),
        P("seq", "fsdp"),
        P("seq", "fsdp"),
        P("seq", "fsdp"),
        P("seq", "fsdp"),
        P("seq", "fsdp"),
        P("seq", None, None),
    )
    out_specs = (
        P("seq", None, "fsdp"),
        P("seq", None, "fsdp"),
        P(None, "seq", None, "fsdp"),
        P("seq", "fsdp"),
        P("seq", "fsdp"),
        P("seq", "fsdp"),
        P("seq", "fsdp"),
        P("seq", "fsdp"),
    )
    return jax.shard_map(body, mesh=mesh, in_specs=in_specs, out_specs=out_specs, check_vma=False)
```

```python
import jax
import jax.numpy as jnp
from jax import lax
from jax.sharding import PartitionSpec as P

HD = 128


epsilon = 1e-06
grad_scale = 0.015625


def layer_norm(hidden):
    average = jnp.mean(hidden, axis=-1, keepdims=True)
    centred = hidden - average
    spread = jnp.mean(centred * centred, axis=-1, keepdims=True)
    return centred * lax.rsqrt(spread + epsilon)


def norm_back(hidden, incoming):
    average = jnp.mean(hidden, axis=-1, keepdims=True)
    centred = hidden - average
    spread = jnp.mean(centred * centred, axis=-1, keepdims=True)
    inverse = lax.rsqrt(spread + epsilon)
    normed = centred * inverse
    return inverse * (
        incoming
        - jnp.mean(incoming, axis=-1, keepdims=True)
        - normed * jnp.mean(incoming * normed, axis=-1, keepdims=True)
    )


def times_t(matrix, factor):
    return lax.dot_general(
        matrix, factor, (((1,), (1,)), ((), ())), preferred_element_type=jnp.float32
    )


def left_times(matrix, factor):
    return (
        lax.dot_general(
            matrix, factor, (((0,), (0,)), ((), ())), preferred_element_type=jnp.float32
        )
        * grad_scale
    )


def attend(query_rows, incoming_keys, value_rows):
    attention_logits = jnp.einsum(
        "otw,osw->ots", query_rows, incoming_keys, preferred_element_type=jnp.float32
    ) * query_rows.shape[-1] ** (-0.5)
    attention_probs = jax.nn.softmax(attention_logits, axis=-1).astype(jnp.bfloat16)
    return jnp.einsum(
        "hfj,hjt->hft", attention_probs, value_rows, preferred_element_type=jnp.float32
    ).astype(jnp.bfloat16)


def spatial(triple):
    frames = triple.shape[1]
    patches = triple.shape[2]
    columns = triple.shape[3]
    heads_here = columns // HD
    pieces = (
        triple.reshape(3, frames, patches, heads_here, HD)
        .transpose(0, 1, 3, 2, 4)
        .reshape(3, frames * heads_here, patches, HD)
    )
    result = attend(pieces[0], pieces[1], pieces[2])
    return (
        result.reshape(frames, heads_here, patches, HD)
        .transpose(0, 2, 1, 3)
        .reshape(frames * patches, columns)
    )


def temporal(triple_rows, frames, spot_count):
    heads_here = triple_rows.shape[1] // (3 * HD)
    pieces = (
        triple_rows.reshape(frames, spot_count, heads_here, 3, HD)
        .transpose(3, 1, 2, 0, 4)
        .reshape(3, spot_count * heads_here, frames, HD)
    )
    result = attend(pieces[0], pieces[1], pieces[2])
    return (
        result.reshape(spot_count, heads_here, frames, HD)
        .transpose(2, 0, 1, 3)
        .reshape(frames * spot_count, heads_here * HD)
    )


def smooth(pre_value):
    return jax.nn.gelu(pre_value, approximate=True)


def fetch_rows(weight):
    return lax.all_gather(weight, "seq", axis=0, tiled=True)


def widen(table):
    copies = jnp.broadcast_to(table[None], (lax.axis_size("fsdp"),) + table.shape)
    return lax.all_to_all(copies, "fsdp", split_axis=0, concat_axis=2, tiled=True)[0]


def head_sum(terms):
    groups = lax.axis_size("fsdp")
    moved = lax.all_to_all(
        terms.astype(jnp.bfloat16), "fsdp", split_axis=1, concat_axis=0, tiled=True
    )
    return jnp.sum(
        moved.reshape(groups, terms.shape[0], terms.shape[1] // groups).astype(jnp.float32), axis=0
    )


def late_sum(terms):
    return lax.psum_scatter(
        terms.astype(jnp.bfloat16), "fsdp", scatter_dimension=1, tiled=True
    ).astype(jnp.float32)


def own_columns(table):
    return lax.all_to_all(table, "seq", split_axis=1, concat_axis=0, tiled=True)


def all_tokens(table):
    return lax.all_gather(table, "seq", axis=0, tiled=True)


def send_rows(grad_part):
    return lax.psum_scatter(
        grad_part.astype(jnp.bfloat16), "seq", scatter_dimension=0, tiled=True
    ).astype(jnp.float32)


def regroup(block):
    return lax.all_to_all(block, "seq", split_axis=0, concat_axis=1, tiled=True)


def to_positions(table, local_frames):
    devices = lax.axis_size("seq")
    row_count = table.shape[0]
    columns = table.shape[1]
    spot_count = row_count // (local_frames * devices)
    block = table.reshape(local_frames, devices, spot_count, columns).transpose(1, 0, 2, 3)
    return regroup(block).reshape(row_count, columns)


def to_frames(table, local_frames):
    devices = lax.axis_size("seq")
    row_count = table.shape[0]
    columns = table.shape[1]
    spot_count = row_count // (local_frames * devices)
    block = table.reshape(devices, local_frames, spot_count, columns)
    moved = regroup(block).reshape(devices, local_frames, spot_count, columns).transpose(1, 0, 2, 3)
    return moved.reshape(row_count, columns)


def body(latents, spatial_qkv, spatial_out, temporal_qkv, temporal_out, mlp_in, mlp_out, upstream):
    local_frames = latents.shape[0]
    patches = latents.shape[1]
    narrow = latents.shape[2]
    devices = lax.axis_size("seq")
    all_frames = local_frames * devices
    spot_count = patches // devices
    row_count = local_frames * patches
    spatial_output, spatial_back = jax.vjp(spatial, spatial_qkv)
    upstream_rows = upstream.reshape(row_count, upstream.shape[2])
    spatial_output, upstream_own = lax.optimization_barrier(
        (spatial_output, own_columns(upstream_rows))
    )
    spatial_full = fetch_rows(spatial_out)
    first_mid = (
        latents.reshape(row_count, narrow).astype(jnp.float32)
        + head_sum(times_t(spatial_output, spatial_full))
    ).astype(jnp.bfloat16)
    first_wide = widen(to_positions(first_mid, local_frames)).astype(jnp.float32)
    first_norm = layer_norm(first_wide).astype(jnp.bfloat16)
    triple_full = fetch_rows(temporal_qkv)
    triple_rows = jnp.dot(first_norm, triple_full, preferred_element_type=jnp.float32).astype(
        jnp.bfloat16
    )
    temporal_result, temporal_back = jax.vjp(
        lambda triple: temporal(triple, all_frames, spot_count), triple_rows
    )
    frames_result = to_frames(temporal_result, local_frames)
    out_full = fetch_rows(temporal_out)
    second_mid = (
        first_mid.astype(jnp.float32) + head_sum(times_t(frames_result, out_full))
    ).astype(jnp.bfloat16)
    second_wide = widen(second_mid).astype(jnp.float32)
    second_norm = layer_norm(second_wide).astype(jnp.bfloat16)
    inner_full = fetch_rows(mlp_in)
    hidden_pre = jnp.dot(second_norm, inner_full, preferred_element_type=jnp.float32)
    hidden_act = smooth(hidden_pre).astype(jnp.bfloat16)
    outer_full = fetch_rows(mlp_out)
    block_out = (second_mid.astype(jnp.float32) + late_sum(times_t(hidden_act, outer_full))).astype(
        jnp.bfloat16
    )
    upstream_rows, first_own, second_own = lax.optimization_barrier(
        (upstream_rows, own_columns(first_norm), own_columns(second_norm))
    )
    hidden_all = all_tokens(hidden_act)
    upstream_cols = lax.dynamic_slice_in_dim(
        upstream_rows, lax.axis_index("fsdp") * narrow, narrow, 1
    )
    act_grad = jnp.dot(upstream_rows, outer_full, preferred_element_type=jnp.float32)
    pre_grad = jax.vjp(smooth, hidden_pre)[1](act_grad)[0].astype(jnp.bfloat16)
    second_grad = (
        upstream_cols.astype(jnp.float32)
        + head_sum(norm_back(second_wide, times_t(pre_grad, inner_full)))
    ).astype(jnp.bfloat16)
    pre_all = all_tokens(pre_grad)
    second_grad_wide, hidden_all = lax.optimization_barrier((widen(second_grad), hidden_all))
    temporal_grad = to_positions(
        jnp.dot(second_grad_wide, out_full, preferred_element_type=jnp.float32).astype(
            jnp.bfloat16
        ),
        local_frames,
    )
    triple_grad = temporal_back(temporal_grad)[0]
    triple_grad, spatial_late = lax.optimization_barrier((triple_grad, spatial_output))
    triple_all = all_tokens(triple_grad)
    spatial_all = all_tokens(spatial_late)
    back_terms, pre_all = lax.optimization_barrier(
        (norm_back(first_wide, times_t(triple_grad, triple_full)).astype(jnp.bfloat16), pre_all)
    )
    first_back = head_sum(back_terms).astype(jnp.bfloat16)
    first_grad = (
        second_grad.astype(jnp.float32) + to_frames(first_back, local_frames).astype(jnp.float32)
    ).astype(jnp.bfloat16)
    first_grad_wide, triple_all = lax.optimization_barrier((widen(first_grad), triple_all))
    spatial_grad = jnp.dot(
        first_grad_wide, spatial_full, preferred_element_type=jnp.float32
    ).astype(jnp.bfloat16)
    grad_spatial_qkv = spatial_back(spatial_grad)[0]
    grads = (
        left_times(own_columns(first_grad_wide), spatial_all),
        left_times(first_own, triple_all),
        send_rows(left_times(second_grad_wide, frames_result)),
        left_times(second_own, pre_all),
        left_times(upstream_own, hidden_all),
    )
    return (
        block_out.reshape(local_frames, patches, narrow),
        first_grad.reshape(local_frames, patches, narrow),
        grad_spatial_qkv,
        grads[0],
        grads[1],
        grads[2],
        grads[3],
        grads[4],
    )


def solution(mesh):
    in_specs = (
        P("seq", None, "fsdp"),
        P(None, "seq", None, "fsdp"),
        P("seq", "fsdp"),
        P("seq", "fsdp"),
        P("seq", "fsdp"),
        P("seq", "fsdp"),
        P("seq", "fsdp"),
        P("seq", None, None),
    )
    out_specs = (
        P("seq", None, "fsdp"),
        P("seq", None, "fsdp"),
        P(None, "seq", None, "fsdp"),
        P("seq", "fsdp"),
        P("seq", "fsdp"),
        P("seq", "fsdp"),
        P("seq", "fsdp"),
        P("seq", "fsdp"),
    )
    return jax.shard_map(body, mesh=mesh, in_specs=in_specs, out_specs=out_specs, check_vma=False)
```

```python
import jax
import jax.numpy as jnp
from jax import lax
from jax.sharding import PartitionSpec as P

HD = 128


epsilon = 1e-06
grad_scale = 0.015625


def layer_norm(hidden):
    average = jnp.mean(hidden, axis=-1, keepdims=True)
    centred = hidden - average
    spread = jnp.mean(centred * centred, axis=-1, keepdims=True)
    return centred * lax.rsqrt(spread + epsilon)


def norm_back(hidden, incoming):
    average = jnp.mean(hidden, axis=-1, keepdims=True)
    centred = hidden - average
    spread = jnp.mean(centred * centred, axis=-1, keepdims=True)
    inverse = lax.rsqrt(spread + epsilon)
    normed = centred * inverse
    return inverse * (
        incoming
        - jnp.mean(incoming, axis=-1, keepdims=True)
        - normed * jnp.mean(incoming * normed, axis=-1, keepdims=True)
    )


def times_t(matrix, factor):
    return lax.dot_general(
        matrix, factor, (((1,), (1,)), ((), ())), preferred_element_type=jnp.float32
    )


def left_times(matrix, factor):
    return (
        lax.dot_general(
            matrix, factor, (((0,), (0,)), ((), ())), preferred_element_type=jnp.float32
        )
        * grad_scale
    )


def attend(query_rows, incoming_keys, value_rows):
    attention_logits = jnp.einsum(
        "otw,osw->ots", query_rows, incoming_keys, preferred_element_type=jnp.float32
    ) * query_rows.shape[-1] ** (-0.5)
    attention_probs = jax.nn.softmax(attention_logits, axis=-1).astype(jnp.bfloat16)
    return jnp.einsum(
        "hfj,hjt->hft", attention_probs, value_rows, preferred_element_type=jnp.float32
    ).astype(jnp.bfloat16)


def spatial(triple):
    frames = triple.shape[1]
    patches = triple.shape[2]
    columns = triple.shape[3]
    heads_here = columns // HD
    pieces = (
        triple.reshape(3, frames, patches, heads_here, HD)
        .transpose(0, 1, 3, 2, 4)
        .reshape(3, frames * heads_here, patches, HD)
    )
    result = attend(pieces[0], pieces[1], pieces[2])
    return (
        result.reshape(frames, heads_here, patches, HD)
        .transpose(0, 2, 1, 3)
        .reshape(frames * patches, columns)
    )


def temporal(triple_rows, frames, spot_count):
    heads_here = triple_rows.shape[1] // (3 * HD)
    pieces = (
        triple_rows.reshape(frames, spot_count, heads_here, 3, HD)
        .transpose(3, 1, 2, 0, 4)
        .reshape(3, spot_count * heads_here, frames, HD)
    )
    result = attend(pieces[0], pieces[1], pieces[2])
    return (
        result.reshape(spot_count, heads_here, frames, HD)
        .transpose(2, 0, 1, 3)
        .reshape(frames * spot_count, heads_here * HD)
    )


def smooth(pre_value):
    return jax.nn.gelu(pre_value, approximate=True)


def fetch_rows(weight):
    return lax.all_gather(weight, "seq", axis=0, tiled=True)


def widen(table):
    copies = jnp.broadcast_to(table[None], (lax.axis_size("fsdp"),) + table.shape)
    return lax.all_to_all(copies, "fsdp", split_axis=0, concat_axis=2, tiled=True)[0]


def head_sum(terms):
    groups = lax.axis_size("fsdp")
    moved = lax.all_to_all(
        terms.astype(jnp.bfloat16), "fsdp", split_axis=1, concat_axis=0, tiled=True
    )
    return jnp.sum(
        moved.reshape(groups, terms.shape[0], terms.shape[1] // groups).astype(jnp.float32), axis=0
    )


def late_sum(terms):
    return lax.psum_scatter(
        terms.astype(jnp.bfloat16), "fsdp", scatter_dimension=1, tiled=True
    ).astype(jnp.float32)


def own_columns(table):
    return lax.all_to_all(table, "seq", split_axis=1, concat_axis=0, tiled=True)


def all_tokens(table):
    return lax.all_gather(table, "seq", axis=0, tiled=True)


def send_rows(grad_part):
    return lax.psum_scatter(
        grad_part.astype(jnp.bfloat16), "seq", scatter_dimension=0, tiled=True
    ).astype(jnp.float32)


def regroup(block):
    return lax.all_to_all(block, "seq", split_axis=0, concat_axis=1, tiled=True)


def to_positions(table, local_frames):
    devices = lax.axis_size("seq")
    row_count = table.shape[0]
    columns = table.shape[1]
    spot_count = row_count // (local_frames * devices)
    block = table.reshape(local_frames, devices, spot_count, columns).transpose(1, 0, 2, 3)
    return regroup(block).reshape(row_count, columns)


def to_frames(table, local_frames):
    devices = lax.axis_size("seq")
    row_count = table.shape[0]
    columns = table.shape[1]
    spot_count = row_count // (local_frames * devices)
    block = table.reshape(devices, local_frames, spot_count, columns)
    moved = regroup(block).reshape(devices, local_frames, spot_count, columns).transpose(1, 0, 2, 3)
    return moved.reshape(row_count, columns)


def body(latents, spatial_qkv, spatial_out, temporal_qkv, temporal_out, mlp_in, mlp_out, upstream):
    local_frames = latents.shape[0]
    patches = latents.shape[1]
    narrow = latents.shape[2]
    devices = lax.axis_size("seq")
    all_frames = local_frames * devices
    spot_count = patches // devices
    row_count = local_frames * patches
    spatial_output, spatial_back = jax.vjp(spatial, spatial_qkv)
    upstream_rows = upstream.reshape(row_count, upstream.shape[2])
    spatial_output, upstream_own = lax.optimization_barrier(
        (spatial_output, own_columns(upstream_rows))
    )
    spatial_full = fetch_rows(spatial_out)
    first_mid = (
        latents.reshape(row_count, narrow).astype(jnp.float32)
        + head_sum(times_t(spatial_output, spatial_full))
    ).astype(jnp.bfloat16)
    first_wide = widen(to_positions(first_mid, local_frames)).astype(jnp.float32)
    first_norm = layer_norm(first_wide).astype(jnp.bfloat16)
    triple_full = fetch_rows(temporal_qkv)
    triple_rows = jnp.dot(first_norm, triple_full, preferred_element_type=jnp.float32).astype(
        jnp.bfloat16
    )
    temporal_result, temporal_back = jax.vjp(
        lambda triple: temporal(triple, all_frames, spot_count), triple_rows
    )
    frames_result = to_frames(temporal_result, local_frames)
    out_full = fetch_rows(temporal_out)
    second_mid = (
        first_mid.astype(jnp.float32) + head_sum(times_t(frames_result, out_full))
    ).astype(jnp.bfloat16)
    second_wide = widen(second_mid).astype(jnp.float32)
    second_norm = layer_norm(second_wide).astype(jnp.bfloat16)
    inner_full = fetch_rows(mlp_in)
    hidden_pre = jnp.dot(second_norm, inner_full, preferred_element_type=jnp.float32)
    hidden_act = smooth(hidden_pre).astype(jnp.bfloat16)
    outer_full = fetch_rows(mlp_out)
    upstream_rows, second_own = lax.optimization_barrier(
        (upstream_rows, own_columns(second_norm))
    )
    hidden_all = all_tokens(hidden_act)
    upstream_cols = lax.dynamic_slice_in_dim(
        upstream_rows, lax.axis_index("fsdp") * narrow, narrow, 1
    )
    act_grad = jnp.dot(upstream_rows, outer_full, preferred_element_type=jnp.float32)
    pre_grad = jax.vjp(smooth, hidden_pre)[1](act_grad)[0].astype(jnp.bfloat16)
    second_grad = (
        upstream_cols.astype(jnp.float32)
        + head_sum(norm_back(second_wide, times_t(pre_grad, inner_full)))
    ).astype(jnp.bfloat16)
    pre_all = all_tokens(pre_grad)
    second_grad_wide, hidden_all = lax.optimization_barrier((widen(second_grad), hidden_all))
    temporal_grad = to_positions(
        jnp.dot(second_grad_wide, out_full, preferred_element_type=jnp.float32).astype(
            jnp.bfloat16
        ),
        local_frames,
    )
    triple_grad = temporal_back(temporal_grad)[0]
    triple_grad, spatial_late, second_late = lax.optimization_barrier(
        (triple_grad, spatial_output, second_grad_wide)
    )
    triple_all = all_tokens(triple_grad)
    spatial_all = all_tokens(spatial_late)
    first_back = head_sum(norm_back(first_wide, times_t(triple_grad, triple_full))).astype(
        jnp.bfloat16
    )
    first_grad = (
        second_grad.astype(jnp.float32) + to_frames(first_back, local_frames).astype(jnp.float32)
    ).astype(jnp.bfloat16)
    first_grad, pre_all = lax.optimization_barrier((first_grad, pre_all))
    first_grad_wide, triple_all, norm_late, hidden_late = lax.optimization_barrier(
        (widen(first_grad), triple_all, first_norm, hidden_act)
    )
    block_out = (
        second_mid.astype(jnp.float32) + late_sum(times_t(hidden_late, outer_full))
    ).astype(jnp.bfloat16)
    spatial_grad = jnp.dot(
        first_grad_wide, spatial_full, preferred_element_type=jnp.float32
    ).astype(jnp.bfloat16)
    grad_spatial_qkv = spatial_back(spatial_grad)[0]
    grads = (
        left_times(own_columns(first_grad_wide), spatial_all),
        left_times(own_columns(norm_late), triple_all),
        send_rows(left_times(second_late, frames_result)),
        left_times(second_own, pre_all),
        left_times(upstream_own, hidden_all),
    )
    return (
        block_out.reshape(local_frames, patches, narrow),
        first_grad.reshape(local_frames, patches, narrow),
        grad_spatial_qkv,
        grads[0],
        grads[1],
        grads[2],
        grads[3],
        grads[4],
    )


def solution(mesh):
    in_specs = (
        P("seq", None, "fsdp"),
        P(None, "seq", None, "fsdp"),
        P("seq", "fsdp"),
        P("seq", "fsdp"),
        P("seq", "fsdp"),
        P("seq", "fsdp"),
        P("seq", "fsdp"),
        P("seq", None, None),
    )
    out_specs = (
        P("seq", None, "fsdp"),
        P("seq", None, "fsdp"),
        P(None, "seq", None, "fsdp"),
        P("seq", "fsdp"),
        P("seq", "fsdp"),
        P("seq", "fsdp"),
        P("seq", "fsdp"),
        P("seq", "fsdp"),
    )
    return jax.shard_map(body, mesh=mesh, in_specs=in_specs, out_specs=out_specs, check_vma=False)
```
